32 devices in a mesh: row: 8 (over y, x, core), col: 4 (over z).
Axes of the slice: x: 2, y: 2, z: 4, core: 2. Of those that a mesh axis runs over, the one named last changes fastest.
Arguments:
- diag_tile: float32 [256, 256], replicated, may hold values from 0 to 10, as said below
- panel_block: float32 [12288, 256], P(('row', 'col')), may hold values from -3 to 3
- trailing: bfloat16 [12288, 12288], P('row', 'col'), may hold values from -6 to 6
- vec_head: float32 [512, 256], P('col'), may hold values from -6 to 6
- vec_rest: float32 [512, 12288], P('col', 'row'), may hold values from -6 to 6
Outputs:
- panel: float32 [12288, 256], P(('row', 'col'))
- trailing_new: bfloat16 [12288, 12288], P('row', 'col')
- whitened: float32 [512, 256], P('col')
- vec_new: float32 [512, 12288], P('col', 'row')
The draws below stay inside these ranges and needn't reach their ends.
Inputs may be any that keep to these rules, and one draw needn't show every extreme that they name: `diag_tile`: symmetric positive definite.
All inputs are finite; a program needn't handle non-finite values.
Results may differ from the reference program's by a relative error of at most 0.0054.
Values may be sent and summed in bfloat16 or wider, within the bound.
No kernel may reach another device: no remote copies, remote signals or barrier semaphores. Data moves between devices by JAX's collectives and lax.ppermute only.
A program may use at most 128 MiB of HBM per device.

```python
import jax
import jax.numpy as jnp
from jax import lax

NB = 256
NVEC = 512
MR = 12288


def draw_diag_tile(key, part):
    sites = jax.random.uniform(jax.random.fold_in(key, 11), (NB, 2), jnp.float32)
    delta_x = sites[:, 0][:, None] - sites[:, 0][None, :]
    delta_y = sites[:, 1][:, None] - sites[:, 1][None, :]
    distance = jnp.sqrt(delta_x * delta_x + delta_y * delta_y)
    length_scale = 0.3
    kernel = jnp.exp(-distance / length_scale)
    base = kernel + 1.5 * jnp.eye(NB, dtype=jnp.float32)
    return base


def level_of(key, shape, shards, smallest, top_value):
    def one(axis_at, parts):
        steps = jax.random.uniform(jax.random.fold_in(jax.random.fold_in(key, 6), axis_at), (parts,), jnp.float32, smallest / len(shards), top_value / len(shards))
        return jnp.repeat(jnp.exp(steps), shape[axis_at] // parts).reshape((-1,) + (1,) * (len(shape) - axis_at - 1))

    factor_of = one(*shards[0])
    for cut in shards[1:]:
        factor_of = factor_of * one(*cut)
    return factor_of


def bell_draw(own_key, extent, deviation, limit, pieces=(), held_as=jnp.bfloat16):
    values = jax.random.normal(own_key, extent, jnp.float32) * deviation
    if len(pieces) > 0:
        values = level_of(own_key, extent, pieces, -0.22, 0.18) * values
    return jnp.clip(values, min=-limit, max=limit).astype(held_as)


def setup_inputs(seed: int = 0) -> dict:
    key_of = jax.random.split(jax.random.key(seed), 6)
    diag_tile = draw_diag_tile(jax.random.fold_in(key_of[5], 71), 0)
    panel_block = bell_draw(key_of[1], (MR, NB), 0.5, 3.0, ((0, 32),), jnp.float32)
    trailing = bell_draw(key_of[2], (MR, MR), 1.0, 6.0, ((0, 8), (1, 4)))
    vec_head = bell_draw(key_of[3], (NVEC, NB), 1.0, 6.0, ((0, 4),), jnp.float32)
    vec_rest = bell_draw(key_of[4], (NVEC, MR), 1.0, 6.0, ((0, 4), (1, 8)), jnp.float32)
    return dict(diag_tile=diag_tile, panel_block=panel_block, trailing=trailing, vec_head=vec_head, vec_rest=vec_rest)


def right_solve(factor, rhs):
    return lax.linalg.triangular_solve(factor, rhs, left_side=False, lower=True, transpose_a=True)

def reference(diag_tile, panel_block, trailing, vec_head, vec_rest):
    factor = jnp.linalg.cholesky(diag_tile)
    panel = right_solve(factor, panel_block)
    panel_half = panel.astype(jnp.bfloat16)
    blocks = trailing.reshape(MR // NB, NB, MR)
    rows_half = panel_half.reshape(MR // NB, NB, NB)

    def update(pair):
        block, rows = pair
        prod = lax.dot_general(rows.astype(jnp.float32), panel_half.astype(jnp.float32), (((1,), (1,)), ((), ())), preferred_element_type=jnp.float32)
        return (block.astype(jnp.float32) - prod).astype(jnp.bfloat16)
    trailing_new = lax.map(update, (blocks, rows_half)).reshape(MR, MR)
    whitened = right_solve(factor, vec_head)
    whitened_half = whitened.astype(jnp.bfloat16)
    prod = lax.dot_general(whitened_half.astype(jnp.float32), panel_half.astype(jnp.float32), (((1,), (1,)), ((), ())), preferred_element_type=jnp.float32)
    vec_new = vec_rest - prod
    return (panel, trailing_new, whitened, vec_new)
```

```python
import functools

import jax
import jax.numpy as jnp
from jax import lax
from jax.experimental import pallas as pl
from jax.experimental.pallas import tpu as pltpu
from jax.sharding import PartitionSpec as P

LANES = 128
SUB = 8
GROUP = 64
EXACT = lax.Precision.HIGHEST


def eliminate(x, first, last):
    n = x.shape[0]
    halves = n // LANES
    sub = lax.broadcasted_iota(jnp.int32, (SUB, LANES), 0)
    lane = lax.broadcasted_iota(jnp.int32, (SUB, LANES), 1)
    count = GROUP // SUB

    def row_of(value, j):
        return jnp.take_along_axis(value, jnp.full((SUB, LANES), j, jnp.int32), axis=0)

    def col_of(value, l):
        return jnp.broadcast_to(value[:, l : l + 1], (SUB, LANES))

    for r0 in range(first, last, GROUP):
        rows = [
            [x[r0 + SUB * g : r0 + SUB * (g + 1), h * LANES : (h + 1) * LANES] for h in range(halves)]
            for g in range(count)
        ]
        ahead = None
        for b in range(count):
            q = r0 + SUB * b
            hq, lq = q // LANES, q % LANES
            cols = {}
            for j in range(SUB):
                cols[b, j] = col_of(rows[b][hq], lq + j) if ahead is None else ahead[j]
            ahead = None
            if b + 1 < count:
                h1, l1 = (q + SUB) // LANES, (q + SUB) % LANES
                for j in range(SUB):
                    cols[b + 1, j] = col_of(rows[b + 1][hq], lq + j)
                ahead = [col_of(rows[b + 1][h1], l1 + j) for j in range(SUB)]
            for g in range(b + 2, count):
                for j in range(SUB):
                    cols[g, j] = col_of(rows[g][hq], lq + j)
            block = (lane >= lq) & (lane < lq + SUB)
            for g in range(b, count):
                rows[g][hq] = jnp.where(block, 0.0, rows[g][hq])
            rows[b][hq] = jnp.where(lane == lq + sub, 1.0, rows[b][hq])
            pivots = None
            for j in range(SUB):
                pivot = row_of(cols[b, j], j)
                inverse = 1.0 / pivot
                pivots = pivot if pivots is None else jnp.where(sub == j, pivot, pivots)
                across = {l: row_of(cols[b, l], j) for l in range(j + 1, SUB)}
                pivot_row = [row_of(rows[b][h], j) for h in range(halves)]
                if ahead is not None:
                    next_row = [row_of(cols[b + 1, j], l) for l in range(SUB)]
                for g in range(b, count):
                    factor = cols[g, j] * inverse
                    if g == b:
                        if j == SUB - 1:
                            continue
                        factor = jnp.where(sub > j, factor, 0.0)
                    for l in range(j + 1, SUB):
                        cols[g, l] = cols[g, l] - factor * across[l]
                    if g == b + 1:
                        for l in range(SUB):
                            ahead[l] = ahead[l] - factor * next_row[l]
                    for h in range(halves):
                        rows[g][h] = rows[g][h] - factor * pivot_row[h]
            scale = lax.rsqrt(pivots)
            for h in range(halves):
                rows[b][h] = rows[b][h] * scale
        for g in range(count):
            for h in range(halves):
                x[r0 + SUB * g : r0 + SUB * (g + 1), h * LANES : (h + 1) * LANES] = rows[g][h]
        r1 = r0 + GROUP
        done = x[r0:r1, :]
        row_at = lax.broadcasted_iota(jnp.int32, (GROUP, n), 0) + r0
        col_at = lax.broadcasted_iota(jnp.int32, (GROUP, n), 1)
        clean = jnp.where((col_at > row_at) & (col_at < r1), 0.0, done)
        for top, bottom in ((r1, min(r1 + GROUP, n)), (min(r1 + GROUP, n), n)):
            if top < bottom:
                update = lax.dot_general(
                    done[:, top:bottom],
                    clean,
                    (((0,), (0,)), ((), ())),
                    precision=EXACT,
                    preferred_element_type=jnp.float32,
                )
                lanes = lax.broadcasted_iota(jnp.int32, (bottom - top, n), 1)
                x[top:bottom, :] = jnp.where((lanes >= r0) & (lanes < r1), 0.0, x[top:bottom, :]) - update


def lower_rows(x, first, last):
    row_at = lax.broadcasted_iota(jnp.int32, (last - first, last), 0) + first
    col_at = lax.broadcasted_iota(jnp.int32, (last - first, last), 1)
    return jnp.where(col_at <= row_at, x[first:last, :last], 0.0)


def times(rhs, inverse):
    return lax.dot_general(
        rhs, inverse, (((1,), (1,)), ((), ())), precision=EXACT, preferred_element_type=jnp.float32
    )


def cost(micros):
    return pl.CostEstimate(flops=int(micros * 1e6), bytes_accessed=int(micros * 1e6), transcendentals=0)


def params(mebibytes):
    return pltpu.CompilerParams(vmem_limit_bytes=mebibytes * 1024 * 1024)


def factor_kernel(diag_ref, panel_ref, inverse_ref, own_ref, x_ref):
    n = diag_ref.shape[0]
    x_ref[...] = diag_ref[...]
    eliminate(x_ref, 0, n)
    inverse = lower_rows(x_ref, 0, n)
    inverse_ref[...] = inverse
    own_ref[...] = times(panel_ref[...], inverse).astype(jnp.bfloat16)


def factor(diag_tile, panel_block):
    return pl.pallas_call(
        factor_kernel,
        out_shape=(
            jax.ShapeDtypeStruct(diag_tile.shape, jnp.float32),
            jax.ShapeDtypeStruct(panel_block.shape, jnp.bfloat16),
        ),
        scratch_shapes=[pltpu.VMEM(diag_tile.shape, jnp.float32)],
        cost_estimate=cost(7),
        compiler_params=params(8),
        name="factor",
    )(*(pltpu.with_memory_space_constraint(v, pltpu.HBM) for v in (diag_tile, panel_block)))


def finish_kernel(inverse_ref, panel_ref, head_ref, rows_ref, rest_ref, panel_out_ref, whitened_ref, rest_out_ref):
    inverse = inverse_ref[...]
    whitened = times(head_ref[...], inverse)
    whitened_ref[...] = whitened
    panel_out_ref[...] = times(panel_ref[...], inverse)
    product = lax.dot_general(
        whitened.astype(jnp.bfloat16), rows_ref[...], (((1,), (1,)), ((), ())), preferred_element_type=jnp.float32
    )
    rest_out_ref[...] = rest_ref[...] - product


def finish(inverse, panel_block, vec_head, rows, vec_rest):
    return pl.pallas_call(
        finish_kernel,
        out_shape=tuple(jax.ShapeDtypeStruct(v.shape, jnp.float32) for v in (panel_block, vec_head, vec_rest)),
        cost_estimate=cost(2),
        compiler_params=params(10),
        name="finish",
    )(inverse, *(pltpu.with_memory_space_constraint(v, pltpu.HBM) for v in (panel_block, vec_head)), rows,
      pltpu.with_memory_space_constraint(vec_rest, pltpu.HBM))


def tile(rows_ref, here, block, old):
    product = lax.dot_general(
        rows_ref[here, :], block, (((1,), (1,)), ((), ())), preferred_element_type=jnp.float32
    )
    return (old.astype(jnp.float32) - product).astype(jnp.bfloat16)


def near_update_kernel(at_ref, rows_ref, mine_ref, other_ref, trailing_ref, out_ref, held_ref, buffer_ref, loaded, stored, fetched):
    chunks = loaded.shape[1]
    height, width = rows_ref.shape[0] // chunks, buffer_ref.shape[2]

    def place(b):
        return pl.ds(pl.multiple_of(at_ref[b] * width, width), width)

    heres = [pl.ds(i * height, height) for i in range(chunks)]
    loads = {
        (b, i): pltpu.make_async_copy(trailing_ref.at[heres[i], place(b)], buffer_ref.at[b, heres[i], :], loaded.at[b, i])
        for b in range(2)
        for i in range(chunks)
    }
    fetches = [
        pltpu.make_async_copy(trailing_ref.at[:, place(2 + b)], held_ref.at[b], fetched.at[b])
        for b in range(held_ref.shape[0])
    ]
    stores = []
    for load in loads.values():
        load.start()
    for fetch in fetches:
        fetch.start()
    for b, cols_ref in enumerate((mine_ref, other_ref)):
        for i in range(chunks):
            loads[b, i].wait()
            buffer_ref[b, heres[i], :] = tile(rows_ref, heres[i], cols_ref[...], buffer_ref[b, heres[i], :])
            stores.append(
                pltpu.make_async_copy(buffer_ref.at[b, heres[i], :], out_ref.at[heres[i], place(b)], stored.at[b, i])
            )
            stores[-1].start()
    for copy in stores + fetches:
        copy.wait()


def near_update(at, rows, mine, other, trailing):
    whole, width, chunks = pl.BlockSpec(memory_space=pltpu.VMEM), mine.shape[0], max(1, rows.shape[0] // 256)
    rest = at.shape[0] - 2
    return pl.pallas_call(
        near_update_kernel,
        in_specs=[pl.BlockSpec(memory_space=pltpu.SMEM), whole, whole, whole, pl.BlockSpec(memory_space=pl.ANY)],
        out_specs=(pl.BlockSpec(memory_space=pl.ANY), whole),
        out_shape=(
            pltpu.HBM(trailing.shape, trailing.dtype),
            pltpu.VMEM((rest, rows.shape[0], width), trailing.dtype),
        ),
        scratch_shapes=[
            pltpu.VMEM((2, rows.shape[0], width), trailing.dtype),
            pltpu.SemaphoreType.DMA((2, chunks)),
            pltpu.SemaphoreType.DMA((2, chunks)),
            pltpu.SemaphoreType.DMA((rest,)),
        ],
        cost_estimate=cost(4),
        compiler_params=params(16),
        name="near_update",
    )(at, rows, mine, other, pltpu.with_memory_space_constraint(trailing, pltpu.HBM))


def far_update_kernel(first, at_ref, rows_ref, cols_ref, held_ref, old_ref, out_ref, buffer_ref, sems):
    blocks, chunks = sems.shape
    height, width = rows_ref.shape[0] // chunks, buffer_ref.shape[2]
    stores = []
    for b in range(blocks):
        place = pl.ds(pl.multiple_of(at_ref[first + b] * width, width), width)
        block = cols_ref[b * width : (b + 1) * width, :]
        for i in range(chunks):
            here = pl.ds(i * height, height)
            buffer_ref[b, here, :] = tile(rows_ref, here, block, held_ref[first + b, here, :])
            stores.append(pltpu.make_async_copy(buffer_ref.at[b, here, :], out_ref.at[here, place], sems.at[b, i]))
            stores[-1].start()
    for store in stores:
        store.wait()


def far_update(first, at, rows, cols, held, out):
    whole, width, chunks = pl.BlockSpec(memory_space=pltpu.VMEM), held.shape[2], max(1, rows.shape[0] // 256)
    blocks = cols.shape[0] // width
    return pl.pallas_call(
        functools.partial(far_update_kernel, first),
        in_specs=[pl.BlockSpec(memory_space=pltpu.SMEM), whole, whole, whole, pl.BlockSpec(memory_space=pl.ANY)],
        out_specs=pl.BlockSpec(memory_space=pl.ANY),
        out_shape=pltpu.HBM(out.shape, out.dtype),
        input_output_aliases={4: 0},
        scratch_shapes=[
            pltpu.VMEM((blocks, rows.shape[0], width), out.dtype),
            pltpu.SemaphoreType.DMA((blocks, chunks)),
        ],
        cost_estimate=cost(1.8 * blocks),
        compiler_params=params(10),
        name="far_update",
    )(at, rows, cols, pltpu.with_memory_space_constraint(held, pltpu.VMEM), out)


def after(value, other):
    return lax.optimization_barrier((value, other))[0]


def flip(value, size, k):
    return lax.ppermute(value, "col", [(c, c ^ k) for c in range(size)])


def swap(value, row_size, col_size):
    moves = [(r * col_size + c, (r ^ 1) * col_size + c) for r in range(row_size) for c in range(col_size)]
    parts = jnp.split(value, 2, axis=0)
    return jnp.concatenate([lax.ppermute(part, ("row", "col"), moves) for part in parts], axis=0)


def spread(mine, row_size, col_size, first_after=(), last_after=()):
    row, col = lax.axis_index("row"), lax.axis_index("col")
    apart = (row // 2) ^ col
    steps = (row_size // 2).bit_length() - 1
    held, have = mine, [[0], [0]]
    for step in range(steps):
        moves, arrived = [], apart < 0
        for i in range(2):
            bit = 1 << ((step + i) % steps)
            for d in have[i]:
                moves += [
                    (((c ^ d) * 2 + i) * col_size + c, ((c ^ d ^ bit) * 2 + i) * col_size + c) for c in range(col_size)
                ]
                arrived = arrived | ((apart == d ^ bit) & (row % 2 == i))
            have[i] = have[i] + [d ^ bit for d in have[i]]
        came = lax.ppermute(held, ("row", "col"), moves)
        if step == 0:
            came = after(came, first_after)
        if step == steps - 1:
            came = after(came, last_after)
        held = jnp.where(arrived, came, held)
    return held


def per_device(row_size, col_size, diag_tile, panel_block, trailing, vec_head, vec_rest):
    row, col = lax.axis_index("row"), lax.axis_index("col")
    odd = (col & 1) == 1
    size = panel_block.shape[0]
    inverse, own = factor(diag_tile, panel_block)
    mate = flip(own, col_size, 1)
    ks = range(2, col_size, 2)
    blocks = {0: own}
    for bit in [1 << i for i in range(1, col_size.bit_length() - 1)][::-1]:
        blocks |= {k ^ bit: flip(v, col_size, bit) for k, v in list(blocks.items())}
    evens = jnp.concatenate([blocks[k] for k in ks], axis=0)
    odds = flip(evens, col_size, 1)

    def paired(a, b):
        count = a.shape[0] // size
        a, b = (v.reshape(count, 1, size, v.shape[1]) for v in (a, b))
        both = jnp.where(odd, jnp.concatenate([b, a], axis=1), jnp.concatenate([a, b], axis=1))
        return both.reshape(2 * count * size, a.shape[3])

    width, count = 2 * size, col_size // 2
    near, far = paired(own, mate), paired(evens, odds)
    rows = jnp.zeros((col_size * size, near.shape[1]), near.dtype)
    for p in range(count):
        pair = near if p == 0 else far[(p - 1) * width : p * width]
        rows = lax.dynamic_update_slice_in_dim(rows, pair, ((col >> 1) ^ p) * width, 0)
    near_cols = spread(near, row_size, col_size)

    def places(offsets):
        values = [((row & 1) ^ half) * (col_size // 2) + ((col >> 1) ^ p) for half in range(2) for p in offsets]
        return jnp.stack(values).astype(jnp.int32)

    far_places = places(range(1, count))
    other_cols = swap(near_cols, row_size, col_size)
    panel, whitened, vec_new = finish(inverse, panel_block, vec_head, rows, vec_rest)
    out, held = near_update(jnp.concatenate([places([0]), far_places]), rows, near_cols, other_cols, trailing)
    far_cols = spread(far, row_size, col_size, vec_new, out)
    out = far_update(0, far_places, rows, far_cols, held, out)
    out = far_update(count - 1, far_places, rows, swap(far_cols, row_size, col_size), held, out)
    return (panel, out, whitened, vec_new)


def solution(mesh):
    row_size, col_size = mesh.shape["row"], mesh.shape["col"]
    in_specs = (P(), P(("row", "col"), None), P("row", "col"), P("col", None), P("col", "row"))
    out_specs = (P(("row", "col"), None), P("row", "col"), P("col", None), P("col", "row"))
    return jax.shard_map(
        functools.partial(per_device, row_size, col_size),
        mesh=mesh,
        in_specs=in_specs,
        out_specs=out_specs,
        check_vma=False,
    )
```

```python
import functools

import jax
import jax.numpy as jnp
from jax import lax
from jax.experimental import pallas as pl
from jax.experimental.pallas import tpu as pltpu
from jax.sharding import PartitionSpec as P

LANES = 128
SUB = 8
GROUP = 64
EXACT = lax.Precision.HIGHEST


def eliminate(x, first, last):
    n = x.shape[0]
    halves = n // LANES
    sub = lax.broadcasted_iota(jnp.int32, (SUB, LANES), 0)
    lane = lax.broadcasted_iota(jnp.int32, (SUB, LANES), 1)
    count = GROUP // SUB

    def row_of(value, j):
        return jnp.take_along_axis(value, jnp.full((SUB, LANES), j, jnp.int32), axis=0)

    def col_of(value, l):
        return jnp.broadcast_to(value[:, l : l + 1], (SUB, LANES))

    for r0 in range(first, last, GROUP):
        rows = [
            [x[r0 + SUB * g : r0 + SUB * (g + 1), h * LANES : (h + 1) * LANES] for h in range(halves)]
            for g in range(count)
        ]
        ahead = None
        for b in range(count):
            q = r0 + SUB * b
            hq, lq = q // LANES, q % LANES
            cols = {}
            for j in range(SUB):
                cols[b, j] = col_of(rows[b][hq], lq + j) if ahead is None else ahead[j]
            ahead = None
            if b + 1 < count:
                h1, l1 = (q + SUB) // LANES, (q + SUB) % LANES
                for j in range(SUB):
                    cols[b + 1, j] = col_of(rows[b + 1][hq], lq + j)
                ahead = [col_of(rows[b + 1][h1], l1 + j) for j in range(SUB)]
            for g in range(b + 2, count):
                for j in range(SUB):
                    cols[g, j] = col_of(rows[g][hq], lq + j)
            block = (lane >= lq) & (lane < lq + SUB)
            for g in range(b, count):
                rows[g][hq] = jnp.where(block, 0.0, rows[g][hq])
            rows[b][hq] = jnp.where(lane == lq + sub, 1.0, rows[b][hq])
            pivots = None
            for j in range(SUB):
                pivot = row_of(cols[b, j], j)
                inverse = 1.0 / pivot
                pivots = pivot if pivots is None else jnp.where(sub == j, pivot, pivots)
                across = {l: row_of(cols[b, l], j) for l in range(j + 1, SUB)}
                pivot_row = [row_of(rows[b][h], j) for h in range(halves)]
                if ahead is not None:
                    next_row = [row_of(cols[b + 1, j], l) for l in range(SUB)]
                for g in range(b, count):
                    factor = cols[g, j] * inverse
                    if g == b:
                        if j == SUB - 1:
                            continue
                        factor = jnp.where(sub > j, factor, 0.0)
                    for l in range(j + 1, SUB):
                        cols[g, l] = cols[g, l] - factor * across[l]
                    if g == b + 1:
                        for l in range(SUB):
                            ahead[l] = ahead[l] - factor * next_row[l]
                    for h in range(halves):
                        rows[g][h] = rows[g][h] - factor * pivot_row[h]
            scale = lax.rsqrt(pivots)
            for h in range(halves):
                rows[b][h] = rows[b][h] * scale
        for g in range(count):
            for h in range(halves):
                x[r0 + SUB * g : r0 + SUB * (g + 1), h * LANES : (h + 1) * LANES] = rows[g][h]
        r1 = r0 + GROUP
        done = x[r0:r1, :]
        row_at = lax.broadcasted_iota(jnp.int32, (GROUP, n), 0) + r0
        col_at = lax.broadcasted_iota(jnp.int32, (GROUP, n), 1)
        clean = jnp.where((col_at > row_at) & (col_at < r1), 0.0, done)
        for top, bottom in ((r1, min(r1 + GROUP, n)), (min(r1 + GROUP, n), n)):
            if top < bottom:
                update = lax.dot_general(
                    done[:, top:bottom],
                    clean,
                    (((0,), (0,)), ((), ())),
                    precision=EXACT,
                    preferred_element_type=jnp.float32,
                )
                lanes = lax.broadcasted_iota(jnp.int32, (bottom - top, n), 1)
                x[top:bottom, :] = jnp.where((lanes >= r0) & (lanes < r1), 0.0, x[top:bottom, :]) - update


def lower_rows(x, first, last):
    row_at = lax.broadcasted_iota(jnp.int32, (last - first, last), 0) + first
    col_at = lax.broadcasted_iota(jnp.int32, (last - first, last), 1)
    return jnp.where(col_at <= row_at, x[first:last, :last], 0.0)


def times(rhs, inverse):
    return lax.dot_general(
        rhs, inverse, (((1,), (1,)), ((), ())), precision=EXACT, preferred_element_type=jnp.float32
    )


def cost(micros):
    return pl.CostEstimate(flops=int(micros * 1e6), bytes_accessed=int(micros * 1e6), transcendentals=0)


def params(mebibytes):
    return pltpu.CompilerParams(vmem_limit_bytes=mebibytes * 1024 * 1024)


def factor_kernel(diag_ref, panel_ref, inverse_ref, own_ref, x_ref):
    n = diag_ref.shape[0]
    x_ref[...] = diag_ref[...]
    eliminate(x_ref, 0, n)
    inverse = lower_rows(x_ref, 0, n)
    inverse_ref[...] = inverse
    own_ref[...] = times(panel_ref[...], inverse).astype(jnp.bfloat16)


def factor(diag_tile, panel_block):
    return pl.pallas_call(
        factor_kernel,
        out_shape=(
            jax.ShapeDtypeStruct(diag_tile.shape, jnp.float32),
            jax.ShapeDtypeStruct(panel_block.shape, jnp.bfloat16),
        ),
        scratch_shapes=[pltpu.VMEM(diag_tile.shape, jnp.float32)],
        cost_estimate=cost(7),
        compiler_params=params(8),
        name="factor",
    )(*(pltpu.with_memory_space_constraint(v, pltpu.HBM) for v in (diag_tile, panel_block)))


def finish_kernel(inverse_ref, panel_ref, head_ref, rows_ref, rest_ref, panel_out_ref, whitened_ref, rest_out_ref):
    inverse = inverse_ref[...]
    whitened = times(head_ref[...], inverse)
    whitened_ref[...] = whitened
    panel_out_ref[...] = times(panel_ref[...], inverse)
    product = lax.dot_general(
        whitened.astype(jnp.bfloat16), rows_ref[...], (((1,), (1,)), ((), ())), preferred_element_type=jnp.float32
    )
    rest_out_ref[...] = rest_ref[...] - product


def finish(inverse, panel_block, vec_head, rows, vec_rest):
    return pl.pallas_call(
        finish_kernel,
        out_shape=tuple(jax.ShapeDtypeStruct(v.shape, jnp.float32) for v in (panel_block, vec_head, vec_rest)),
        cost_estimate=cost(2),
        compiler_params=params(10),
        name="finish",
    )(inverse, *(pltpu.with_memory_space_constraint(v, pltpu.HBM) for v in (panel_block, vec_head)), rows,
      pltpu.with_memory_space_constraint(vec_rest, pltpu.HBM))


def tile(rows_ref, here, block, old):
    product = lax.dot_general(
        rows_ref[here, :], block, (((1,), (1,)), ((), ())), preferred_element_type=jnp.float32
    )
    return (old.astype(jnp.float32) - product).astype(jnp.bfloat16)


def near_update_kernel(at_ref, rows_ref, mine_ref, other_ref, trailing_ref, out_ref, held_ref, buffer_ref, loaded, stored, fetched):
    chunks = loaded.shape[1]
    height, width = rows_ref.shape[0] // chunks, buffer_ref.shape[2]

    def place(b):
        return pl.ds(pl.multiple_of(at_ref[b] * width, width), width)

    heres = [pl.ds(i * height, height) for i in range(chunks)]
    loads = {
        (b, i): pltpu.make_async_copy(trailing_ref.at[heres[i], place(b)], buffer_ref.at[b, heres[i], :], loaded.at[b, i])
        for b in range(2)
        for i in range(chunks)
    }
    fetches = [
        pltpu.make_async_copy(
            trailing_ref.at[:, place(2 + b)], held_ref.at[:, pl.ds(b * width, width)], fetched.at[b]
        )
        for b in range(fetched.shape[0])
    ]
    stores = []
    for load in loads.values():
        load.start()
    for fetch in fetches:
        fetch.start()
    for b, cols_ref in enumerate((mine_ref, other_ref)):
        for i in range(chunks):
            loads[b, i].wait()
            buffer_ref[b, heres[i], :] = tile(rows_ref, heres[i], cols_ref[...], buffer_ref[b, heres[i], :])
            stores.append(
                pltpu.make_async_copy(buffer_ref.at[b, heres[i], :], out_ref.at[heres[i], place(b)], stored.at[b, i])
            )
            stores[-1].start()
    for copy in stores + fetches:
        copy.wait()


def near_update(at, rows, mine, other, trailing):
    whole, width, chunks = pl.BlockSpec(memory_space=pltpu.VMEM), mine.shape[0], max(1, rows.shape[0] // 512)
    rest = at.shape[0] - 2
    return pl.pallas_call(
        near_update_kernel,
        in_specs=[pl.BlockSpec(memory_space=pltpu.SMEM), whole, whole, whole, pl.BlockSpec(memory_space=pl.ANY)],
        out_specs=(pl.BlockSpec(memory_space=pl.ANY), whole),
        out_shape=(
            pltpu.HBM(trailing.shape, trailing.dtype),
            pltpu.VMEM((rows.shape[0], rest * width), trailing.dtype),
        ),
        scratch_shapes=[
            pltpu.VMEM((2, rows.shape[0], width), trailing.dtype),
            pltpu.SemaphoreType.DMA((2, chunks)),
            pltpu.SemaphoreType.DMA((2, chunks)),
            pltpu.SemaphoreType.DMA((rest,)),
        ],
        cost_estimate=cost(4),
        compiler_params=params(16),
        name="near_update",
    )(at, rows, mine, other, pltpu.with_memory_space_constraint(trailing, pltpu.HBM))


def far_update_kernel(first, at_ref, rows_ref, cols_ref, held_ref, old_ref, out_ref, buffer_ref, sems):
    blocks, chunks = sems.shape
    height, width = rows_ref.shape[0] // chunks, buffer_ref.shape[2]
    stores = []
    for b in range(blocks):
        place = pl.ds(pl.multiple_of(at_ref[first + b] * width, width), width)
        block = cols_ref[b * width : (b + 1) * width, :]
        for i in range(chunks):
            here = pl.ds(i * height, height)
            buffer_ref[b, here, :] = tile(rows_ref, here, block, held_ref[here, (first + b) * width : (first + b + 1) * width])
            stores.append(pltpu.make_async_copy(buffer_ref.at[b, here, :], out_ref.at[here, place], sems.at[b, i]))
            stores[-1].start()
    for store in stores:
        store.wait()


def far_update(first, at, rows, cols, held, out):
    whole, chunks = pl.BlockSpec(memory_space=pltpu.VMEM), max(1, rows.shape[0] // 256)
    width = held.shape[1] // (at.shape[0])
    blocks = cols.shape[0] // width
    return pl.pallas_call(
        functools.partial(far_update_kernel, first),
        in_specs=[pl.BlockSpec(memory_space=pltpu.SMEM), whole, whole, whole, pl.BlockSpec(memory_space=pl.ANY)],
        out_specs=pl.BlockSpec(memory_space=pl.ANY),
        out_shape=pltpu.HBM(out.shape, out.dtype),
        input_output_aliases={4: 0},
        scratch_shapes=[
            pltpu.VMEM((blocks, rows.shape[0], width), out.dtype),
            pltpu.SemaphoreType.DMA((blocks, chunks)),
        ],
        cost_estimate=cost(1.8 * blocks),
        compiler_params=params(10),
        name="far_update",
    )(at, rows, cols, pltpu.with_memory_space_constraint(held, pltpu.VMEM), out)


def after(value, other):
    return lax.optimization_barrier((value, other))[0]


def flip(value, size, k):
    return lax.ppermute(value, "col", [(c, c ^ k) for c in range(size)])


def swap(value, row_size, col_size):
    moves = [(r * col_size + c, (r ^ 1) * col_size + c) for r in range(row_size) for c in range(col_size)]
    parts = jnp.split(value, 2, axis=0)
    return jnp.concatenate([lax.ppermute(part, ("row", "col"), moves) for part in parts], axis=0)


def spread(mine, row_size, col_size, first_after=(), last_after=()):
    row, col = lax.axis_index("row"), lax.axis_index("col")
    apart = (row // 2) ^ col
    steps = (row_size // 2).bit_length() - 1
    held, have = mine, [[0], [0]]
    for step in range(steps):
        moves, arrived = [], apart < 0
        for i in range(2):
            bit = 1 << ((step + i) % steps)
            for d in have[i]:
                moves += [
                    (((c ^ d) * 2 + i) * col_size + c, ((c ^ d ^ bit) * 2 + i) * col_size + c) for c in range(col_size)
                ]
                arrived = arrived | ((apart == d ^ bit) & (row % 2 == i))
            have[i] = have[i] + [d ^ bit for d in have[i]]
        came = lax.ppermute(held, ("row", "col"), moves)
        if step == 0:
            came = after(came, first_after)
        if step == steps - 1:
            came = after(came, last_after)
        held = jnp.where(arrived, came, held)
    return held


def per_device(row_size, col_size, diag_tile, panel_block, trailing, vec_head, vec_rest):
    row, col = lax.axis_index("row"), lax.axis_index("col")
    odd = (col & 1) == 1
    size = panel_block.shape[0]
    inverse, own = factor(diag_tile, panel_block)
    mate = flip(own, col_size, 1)
    ks = range(2, col_size, 2)
    blocks = {0: own}
    for bit in [1 << i for i in range(1, col_size.bit_length() - 1)][::-1]:
        blocks |= {k ^ bit: flip(v, col_size, bit) for k, v in list(blocks.items())}
    evens = jnp.concatenate([blocks[k] for k in ks], axis=0)
    odds = flip(evens, col_size, 1)

    def paired(a, b):
        count = a.shape[0] // size
        a, b = (v.reshape(count, 1, size, v.shape[1]) for v in (a, b))
        both = jnp.where(odd, jnp.concatenate([b, a], axis=1), jnp.concatenate([a, b], axis=1))
        return both.reshape(2 * count * size, a.shape[3])

    width, count = 2 * size, col_size // 2
    near, far = paired(own, mate), paired(evens, odds)
    rows = jnp.zeros((col_size * size, near.shape[1]), near.dtype)
    for p in range(count):
        pair = near if p == 0 else far[(p - 1) * width : p * width]
        rows = lax.dynamic_update_slice_in_dim(rows, pair, ((col >> 1) ^ p) * width, 0)
    near_cols = spread(near, row_size, col_size)

    def places(offsets):
        values = [((row & 1) ^ half) * (col_size // 2) + ((col >> 1) ^ p) for half in range(2) for p in offsets]
        return jnp.stack(values).astype(jnp.int32)

    far_places = places(range(1, count))
    other_cols = swap(near_cols, row_size, col_size)
    panel, whitened, vec_new = finish(inverse, panel_block, vec_head, rows, vec_rest)
    out, held = near_update(jnp.concatenate([places([0]), far_places]), rows, near_cols, other_cols, trailing)
    far_cols = spread(far, row_size, col_size, vec_new, out)
    out = far_update(0, far_places, rows, far_cols, held, out)
    out = far_update(count - 1, far_places, rows, swap(far_cols, row_size, col_size), held, out)
    return (panel, out, whitened, vec_new)


def solution(mesh):
    row_size, col_size = mesh.shape["row"], mesh.shape["col"]
    in_specs = (P(), P(("row", "col"), None), P("row", "col"), P("col", None), P("col", "row"))
    out_specs = (P(("row", "col"), None), P("row", "col"), P("col", None), P("col", "row"))
    return jax.shard_map(
        functools.partial(per_device, row_size, col_size),
        mesh=mesh,
        in_specs=in_specs,
        out_specs=out_specs,
        check_vma=False,
    )
```

```python
import functools

import jax
import jax.numpy as jnp
from jax import lax
from jax.experimental import pallas as pl
from jax.experimental.pallas import tpu as pltpu
from jax.sharding import PartitionSpec as P

LANES = 128
SUB = 8
GROUP = 64
EXACT = lax.Precision.HIGHEST


def eliminate(x, first, last):
    n = x.shape[0]
    halves = n // LANES
    sub = lax.broadcasted_iota(jnp.int32, (SUB, LANES), 0)
    lane = lax.broadcasted_iota(jnp.int32, (SUB, LANES), 1)
    count = GROUP // SUB

    def row_of(value, j):
        return jnp.take_along_axis(value, jnp.full((SUB, LANES), j, jnp.int32), axis=0)

    def col_of(value, l):
        return jnp.broadcast_to(value[:, l : l + 1], (SUB, LANES))

    for r0 in range(first, last, GROUP):
        rows = [
            [x[r0 + SUB * g : r0 + SUB * (g + 1), h * LANES : (h + 1) * LANES] for h in range(halves)]
            for g in range(count)
        ]
        ahead = None
        for b in range(count):
            q = r0 + SUB * b
            hq, lq = q // LANES, q % LANES
            cols = {}
            for j in range(SUB):
                cols[b, j] = col_of(rows[b][hq], lq + j) if ahead is None else ahead[j]
            ahead = None
            if b + 1 < count:
                h1, l1 = (q + SUB) // LANES, (q + SUB) % LANES
                for j in range(SUB):
                    cols[b + 1, j] = col_of(rows[b + 1][hq], lq + j)
                ahead = [col_of(rows[b + 1][h1], l1 + j) for j in range(SUB)]
            for g in range(b + 2, count):
                for j in range(SUB):
                    cols[g, j] = col_of(rows[g][hq], lq + j)
            block = (lane >= lq) & (lane < lq + SUB)
            for g in range(b, count):
                rows[g][hq] = jnp.where(block, 0.0, rows[g][hq])
            rows[b][hq] = jnp.where(lane == lq + sub, 1.0, rows[b][hq])
            pivots = None
            for j in range(SUB):
                pivot = row_of(cols[b, j], j)
                inverse = 1.0 / pivot
                pivots = pivot if pivots is None else jnp.where(sub == j, pivot, pivots)
                across = {l: row_of(cols[b, l], j) for l in range(j + 1, SUB)}
                pivot_row = [row_of(rows[b][h], j) for h in range(halves)]
                if ahead is not None:
                    next_row = [row_of(cols[b + 1, j], l) for l in range(SUB)]
                for g in range(b, count):
                    factor = cols[g, j] * inverse
                    if g == b:
                        if j == SUB - 1:
                            continue
                        factor = jnp.where(sub > j, factor, 0.0)
                    for l in range(j + 1, SUB):
                        cols[g, l] = cols[g, l] - factor * across[l]
                    if g == b + 1:
                        for l in range(SUB):
                            ahead[l] = ahead[l] - factor * next_row[l]
                    for h in range(halves):
                        rows[g][h] = rows[g][h] - factor * pivot_row[h]
            scale = lax.rsqrt(pivots)
            for h in range(halves):
                rows[b][h] = rows[b][h] * scale
        for g in range(count):
            for h in range(halves):
                x[r0 + SUB * g : r0 + SUB * (g + 1), h * LANES : (h + 1) * LANES] = rows[g][h]
        r1 = r0 + GROUP
        done = x[r0:r1, :]
        row_at = lax.broadcasted_iota(jnp.int32, (GROUP, n), 0) + r0
        col_at = lax.broadcasted_iota(jnp.int32, (GROUP, n), 1)
        clean = jnp.where((col_at > row_at) & (col_at < r1), 0.0, done)
        for top, bottom in ((r1, min(r1 + GROUP, n)), (min(r1 + GROUP, n), n)):
            if top < bottom:
                update = lax.dot_general(
                    done[:, top:bottom],
                    clean,
                    (((0,), (0,)), ((), ())),
                    precision=EXACT,
                    preferred_element_type=jnp.float32,
                )
                lanes = lax.broadcasted_iota(jnp.int32, (bottom - top, n), 1)
                x[top:bottom, :] = jnp.where((lanes >= r0) & (lanes < r1), 0.0, x[top:bottom, :]) - update


def lower_rows(x, first, last):
    row_at = lax.broadcasted_iota(jnp.int32, (last - first, last), 0) + first
    col_at = lax.broadcasted_iota(jnp.int32, (last - first, last), 1)
    return jnp.where(col_at <= row_at, x[first:last, :last], 0.0)


def times(rhs, inverse):
    return lax.dot_general(
        rhs, inverse, (((1,), (1,)), ((), ())), precision=EXACT, preferred_element_type=jnp.float32
    )


def cost(micros):
    return pl.CostEstimate(flops=int(micros * 1e6), bytes_accessed=int(micros * 1e6), transcendentals=0)


def params(mebibytes):
    return pltpu.CompilerParams(vmem_limit_bytes=mebibytes * 1024 * 1024)


def factor_kernel(diag_ref, panel_ref, inverse_ref, own_ref, x_ref):
    n = diag_ref.shape[0]
    x_ref[...] = diag_ref[...]
    eliminate(x_ref, 0, n)
    inverse = lower_rows(x_ref, 0, n)
    inverse_ref[...] = inverse
    own_ref[...] = times(panel_ref[...], inverse).astype(jnp.bfloat16)


def factor(diag_tile, panel_block):
    return pl.pallas_call(
        factor_kernel,
        out_shape=(
            jax.ShapeDtypeStruct(diag_tile.shape, jnp.float32),
            jax.ShapeDtypeStruct(panel_block.shape, jnp.bfloat16),
        ),
        scratch_shapes=[pltpu.VMEM(diag_tile.shape, jnp.float32)],
        cost_estimate=cost(7),
        compiler_params=params(8),
        name="factor",
    )(*(pltpu.with_memory_space_constraint(v, pltpu.HBM) for v in (diag_tile, panel_block)))


def finish_kernel(inverse_ref, panel_ref, head_ref, rows_ref, rest_ref, panel_out_ref, whitened_ref, rest_out_ref):
    inverse = inverse_ref[...]
    whitened = times(head_ref[...], inverse)
    whitened_ref[...] = whitened
    panel_out_ref[...] = times(panel_ref[...], inverse)
    product = lax.dot_general(
        whitened.astype(jnp.bfloat16), rows_ref[...], (((1,), (1,)), ((), ())), preferred_element_type=jnp.float32
    )
    rest_out_ref[...] = rest_ref[...] - product


def finish(inverse, panel_block, vec_head, rows, vec_rest):
    return pl.pallas_call(
        finish_kernel,
        out_shape=tuple(jax.ShapeDtypeStruct(v.shape, jnp.float32) for v in (panel_block, vec_head, vec_rest)),
        cost_estimate=cost(2),
        compiler_params=params(10),
        name="finish",
    )(inverse, *(pltpu.with_memory_space_constraint(v, pltpu.HBM) for v in (panel_block, vec_head)), rows,
      pltpu.with_memory_space_constraint(vec_rest, pltpu.HBM))


def tile(rows_ref, here, block, old):
    product = lax.dot_general(
        rows_ref[here, :], block, (((1,), (1,)), ((), ())), preferred_element_type=jnp.float32
    )
    return (old.astype(jnp.float32) - product).astype(jnp.bfloat16)


def near_update_kernel(at_ref, rows_ref, mine_ref, other_ref, trailing_ref, out_ref, held_ref, buffer_ref, loaded, stored, fetched):
    chunks = loaded.shape[1]
    height, width = rows_ref.shape[0] // chunks, buffer_ref.shape[2]

    def place(b):
        return pl.ds(pl.multiple_of(at_ref[b] * width, width), width)

    heres = [pl.ds(i * height, height) for i in range(chunks)]
    loads = {
        (b, i): pltpu.make_async_copy(trailing_ref.at[heres[i], place(b)], buffer_ref.at[b, heres[i], :], loaded.at[b, i])
        for b in range(2)
        for i in range(chunks)
    }
    fetches = [
        pltpu.make_async_copy(
            trailing_ref.at[:, place(2 + b)], held_ref.at[:, pl.ds(b * width, width)], fetched.at[b]
        )
        for b in range(fetched.shape[0])
    ]
    stores = []
    for load in loads.values():
        load.start()
    for fetch in fetches:
        fetch.start()
    for b, cols_ref in enumerate((mine_ref, other_ref)):
        for i in range(chunks):
            loads[b, i].wait()
            buffer_ref[b, heres[i], :] = tile(rows_ref, heres[i], cols_ref[...], buffer_ref[b, heres[i], :])
            stores.append(
                pltpu.make_async_copy(buffer_ref.at[b, heres[i], :], out_ref.at[heres[i], place(b)], stored.at[b, i])
            )
            stores[-1].start()
    for copy in stores + fetches:
        copy.wait()


def near_update(at, rows, mine, other, trailing):
    whole, width, chunks = pl.BlockSpec(memory_space=pltpu.VMEM), mine.shape[0], max(1, rows.shape[0] // 512)
    rest = at.shape[0] - 2
    return pl.pallas_call(
        near_update_kernel,
        in_specs=[pl.BlockSpec(memory_space=pltpu.SMEM), whole, whole, whole, pl.BlockSpec(memory_space=pl.ANY)],
        out_specs=(pl.BlockSpec(memory_space=pl.ANY), whole),
        out_shape=(
            pltpu.HBM(trailing.shape, trailing.dtype),
            pltpu.VMEM((rows.shape[0], rest * width), trailing.dtype),
        ),
        scratch_shapes=[
            pltpu.VMEM((2, rows.shape[0], width), trailing.dtype),
            pltpu.SemaphoreType.DMA((2, chunks)),
            pltpu.SemaphoreType.DMA((2, chunks)),
            pltpu.SemaphoreType.DMA((rest,)),
        ],
        cost_estimate=cost(4),
        compiler_params=params(16),
        name="near_update",
    )(at, rows, mine, other, pltpu.with_memory_space_constraint(trailing, pltpu.HBM))


def far_update_kernel(first, at_ref, rows_ref, cols_ref, held_ref, old_ref, out_ref, buffer_ref, sems):
    blocks, chunks = sems.shape
    height, width = rows_ref.shape[0] // chunks, buffer_ref.shape[2]
    stores = []
    for b in range(blocks):
        place = pl.ds(pl.multiple_of(at_ref[first + b] * width, width), width)
        block = cols_ref[b * width : (b + 1) * width, :]
        for i in range(chunks):
            here = pl.ds(i * height, height)
            buffer_ref[b, here, :] = tile(rows_ref, here, block, held_ref[here, (first + b) * width : (first + b + 1) * width])
            stores.append(pltpu.make_async_copy(buffer_ref.at[b, here, :], out_ref.at[here, place], sems.at[b, i]))
            stores[-1].start()
    for store in stores:
        store.wait()


def far_update(first, at, rows, cols, held, out):
    whole, chunks = pl.BlockSpec(memory_space=pltpu.VMEM), max(1, rows.shape[0] // 256)
    width = held.shape[1] // (at.shape[0])
    blocks = cols.shape[0] // width
    return pl.pallas_call(
        functools.partial(far_update_kernel, first),
        in_specs=[pl.BlockSpec(memory_space=pltpu.SMEM), whole, whole, whole, pl.BlockSpec(memory_space=pl.ANY)],
        out_specs=pl.BlockSpec(memory_space=pl.ANY),
        out_shape=pltpu.HBM(out.shape, out.dtype),
        input_output_aliases={4: 0},
        scratch_shapes=[
            pltpu.VMEM((blocks, rows.shape[0], width), out.dtype),
            pltpu.SemaphoreType.DMA((blocks, chunks)),
        ],
        cost_estimate=cost(1.8 * blocks),
        compiler_params=params(10),
        name="far_update",
    )(at, rows, cols, pltpu.with_memory_space_constraint(held, pltpu.VMEM), out)


def after(value, other):
    return lax.optimization_barrier((value, other))[0]


def flip(value, size, k):
    return lax.ppermute(value, "col", [(c, c ^ k) for c in range(size)])


def swap(value, row_size, col_size):
    moves = [(r * col_size + c, (r ^ 1) * col_size + c) for r in range(row_size) for c in range(col_size)]
    parts = [value]
    return jnp.concatenate([lax.ppermute(part, ("row", "col"), moves) for part in parts], axis=0)


def spread(mine, row_size, col_size, first_after=(), last_after=()):
    row, col = lax.axis_index("row"), lax.axis_index("col")
    apart = (row // 2) ^ col
    steps = (row_size // 2).bit_length() - 1
    held, have = mine, [[0], [0]]
    for step in range(steps):
        moves, arrived = [], apart < 0
        for i in range(2):
            bit = 1 << ((step + i) % steps)
            for d in have[i]:
                moves += [
                    (((c ^ d) * 2 + i) * col_size + c, ((c ^ d ^ bit) * 2 + i) * col_size + c) for c in range(col_size)
                ]
                arrived = arrived | ((apart == d ^ bit) & (row % 2 == i))
            have[i] = have[i] + [d ^ bit for d in have[i]]
        came = lax.ppermute(held, ("row", "col"), moves)
        if step == 0:
            came = after(came, first_after)
        if step == steps - 1:
            came = after(came, last_after)
        held = jnp.where(arrived, came, held)
    return held


def per_device(row_size, col_size, diag_tile, panel_block, trailing, vec_head, vec_rest):
    row, col = lax.axis_index("row"), lax.axis_index("col")
    odd = (col & 1) == 1
    size = panel_block.shape[0]
    inverse, own = factor(diag_tile, panel_block)
    mate = flip(own, col_size, 1)
    ks = range(2, col_size, 2)
    blocks = {0: own}
    for bit in [1 << i for i in range(1, col_size.bit_length() - 1)][::-1]:
        blocks |= {k ^ bit: flip(v, col_size, bit) for k, v in list(blocks.items())}
    evens = jnp.concatenate([blocks[k] for k in ks], axis=0)
    odds = flip(evens, col_size, 1)

    def paired(a, b):
        count = a.shape[0] // size
        a, b = (v.reshape(count, 1, size, v.shape[1]) for v in (a, b))
        both = jnp.where(odd, jnp.concatenate([b, a], axis=1), jnp.concatenate([a, b], axis=1))
        return both.reshape(2 * count * size, a.shape[3])

    width, count = 2 * size, col_size // 2
    near, far = paired(own, mate), paired(evens, odds)
    rows = jnp.zeros((col_size * size, near.shape[1]), near.dtype)
    for p in range(count):
        pair = near if p == 0 else far[(p - 1) * width : p * width]
        rows = lax.dynamic_update_slice_in_dim(rows, pair, ((col >> 1) ^ p) * width, 0)
    near_cols = spread(near, row_size, col_size)

    def places(offsets):
        values = [((row & 1) ^ half) * (col_size // 2) + ((col >> 1) ^ p) for half in range(2) for p in offsets]
        return jnp.stack(values).astype(jnp.int32)

    far_places = places(range(1, count))
    other_cols = swap(near_cols, row_size, col_size)
    panel, whitened, vec_new = finish(inverse, panel_block, vec_head, rows, vec_rest)
    out, held = near_update(jnp.concatenate([places([0]), far_places]), rows, near_cols, other_cols, trailing)
    far_cols = spread(far, row_size, col_size, vec_new, out)
    out = far_update(0, far_places, rows, far_cols, held, out)
    out = far_update(count - 1, far_places, rows, swap(far_cols, row_size, col_size), held, out)
    return (panel, out, whitened, vec_new)


def solution(mesh):
    row_size, col_size = mesh.shape["row"], mesh.shape["col"]
    in_specs = (P(), P(("row", "col"), None), P("row", "col"), P("col", None), P("col", "row"))
    out_specs = (P(("row", "col"), None), P("row", "col"), P("col", None), P("col", "row"))
    return jax.shard_map(
        functools.partial(per_device, row_size, col_size),
        mesh=mesh,
        in_specs=in_specs,
        out_specs=out_specs,
        check_vma=False,
    )
```
